32 devices in a mesh: gx: 16 (over z, y, x), gy: 2 (over core).
Axes of the slice: x: 2, y: 2, z: 4, core: 2. Of those that a mesh axis runs over, the one named last changes fastest.
Arguments:
- positions: float32 [3, 2, 139264], P(None, 'gy', 'gx'), may hold values from -7 to 7
- forces: float32 [3, 2, 139264], P(None, 'gy', 'gx'), may hold values from -6 to 6
- deriv_mat: float32 [544, 544], replicated, may hold values from -0.25 to 0.25
- quad_mat: float32 [544, 544], replicated, may hold values from -0.25 to 0.25
- point_dest: int32 [2, 139264], P('gy', 'gx'), may hold values from 0 to 32767, as said below
- leaf_center: float32 [3, 2, 4096], P(None, 'gy', 'gx'), may hold values from -4 to 4
- tile_src: int32 [2, 524288], P('gy', 'gx'), may hold values from 0 to 32768, as said below
- neighbours: int32 [2, 3, 4096], P('gy', None, 'gx'), may hold values from 0 to 4095, as said below
- inter_leaf: int32 [2, 8, 4096], P('gy', None, 'gx'), may hold values from 0 to 4095, as said below
- inter_op: int32 [2, 8, 4096], P('gy', None, 'gx'), may hold values from 0 to 15
- coarse_op: int32 [2, 16, 32], P('gy', 'gx'), may hold values from 0 to 16, as said below
- up_pinv: float32 [168, 168], replicated, may hold values from -0.5 to 0.5
- trans_ops: float32 [16, 168, 168], replicated, may hold values from -0.25 to 0.25
- child_ops: float32 [8, 168, 168], replicated, may hold values from -0.03125 to 0.03125
Outputs:
- velocity: float32 [3, 2, 139264], P(None, 'gy', 'gx')
The draws below stay inside these ranges and needn't reach their ends.
Inputs may be any that keep to these rules, and one draw needn't show every extreme that they name: `point_dest`: within one slab and one column block d, the values are distinct; the slots sent to each owner are used from k = 0 without gaps; every column block fills all 2048 slots of the same 16 // 8 owners. `tile_src`: each point of the slab fills exactly one leaf slot of the owner it is sent to; 32768 marks an empty slot; the busiest owners have all slots filled. `neighbours`: entry 0 is the leaf itself; the others lie within 256 leaves of it. `inter_leaf`: every entry lies within 256 leaves of its leaf. `coarse_op`: 16 marks no interaction; it stands exactly for the target box itself and the boxes of the owners next to it in the same slab.
All inputs are finite; a program needn't handle non-finite values.
Results may differ from the reference program's by a relative error of at most 0.0003.
Values sent between devices are 32-bit elements; how exact they have to be, the bound alone decides.
A program may use at most 192 MiB of HBM per device.

```python
import math
import jax
import jax.numpy as jnp
from jax import lax

P_SIZE = 544
EXP = 168
SURF = 56
NOPS = 16
TILE = 128
K_NB = 3
K_IL = 8
L_DEV = 256
CAP = 2048
NPD = 8704
NPS = 139264
NLS = 4096
N_GX = 16
N_GY = 2


def slab_routing(key):
    nbusy = N_GX // 8
    nrest = N_GX - nbusy
    rest_points = NPD - nbusy * CAP
    base = rest_points // nrest
    extra = rest_points % nrest
    key_busy, key_send, key_take = jax.random.split(key, 3)
    owner_rank = jax.random.permutation(key_busy, N_GX)
    busy = owner_rank < nbusy
    rest_position = jnp.clip(jnp.cumsum((~busy).astype(jnp.int32)) - 1, 0, nrest - 1)

    def counts_for(single):
        order = jax.random.permutation(single, nrest)
        return jnp.where(busy, CAP, base + (order[rest_position] < extra).astype(jnp.int32)).astype(jnp.int32)
    send_keys = jax.random.split(key_send, N_GX)
    counts = jax.vmap(counts_for)(send_keys)

    def dest_for(single, count_row):
        inclusive = jnp.cumsum(count_row)
        exclusive = inclusive - count_row
        ranks = jnp.arange(NPD, dtype=jnp.int32)
        owner = jnp.searchsorted(inclusive, ranks, side='right').astype(jnp.int32)
        within = ranks - exclusive[owner]
        shuffle = jax.random.permutation(jax.random.fold_in(single, 7), NPD)
        return jnp.zeros((NPD,), jnp.int32).at[shuffle].set(owner * CAP + within)
    dest = jax.vmap(dest_for)(send_keys, counts)

    def tiles_for(single, count_col):
        flat = jnp.arange(N_GX * CAP, dtype=jnp.int32)
        valid = flat % CAP < count_col[flat // CAP]
        rank = jnp.clip(jnp.cumsum(valid.astype(jnp.int32)) - 1, 0, L_DEV * TILE - 1)
        slot_order = jax.random.permutation(single, L_DEV * TILE)
        target = jnp.where(valid, slot_order[rank], L_DEV * TILE).astype(jnp.int32)
        source = jnp.full((L_DEV * TILE,), N_GX * CAP, jnp.int32).at[target].set(flat, mode='drop')
        return (source, jnp.where(valid, target, 0).astype(jnp.int32))
    take_keys = jax.random.split(key_take, N_GX)
    source, slot_of = jax.vmap(tiles_for)(take_keys, counts.T)
    owner = dest // CAP
    within = dest % CAP
    sender = jnp.arange(N_GX, dtype=jnp.int32)[:, None]
    slot = slot_of[owner, sender * CAP + within]
    leaf = owner * L_DEV + slot // TILE
    return (dest.reshape(-1), source.reshape(-1), leaf.reshape(-1))


def all_routing(key):
    keys = jax.random.split(jax.random.fold_in(key, 101), N_GY)
    return jax.vmap(slab_routing)(keys)


def center_table(key):
    center_key = jax.random.fold_in(key, 202)
    return jax.random.uniform(center_key, (3, N_GY, NLS), jnp.float32, -4.0, 4.0)


def draw_point_dest(key, part):
    return all_routing(key)[0]


def draw_tile_src(key, part):
    return all_routing(key)[1]


def draw_leaf_center(key, part):
    return center_table(key)


def draw_positions(key, part):
    centers = center_table(key)
    leaf = all_routing(key)[2]
    offset_key = jax.random.fold_in(key, 303)
    offset = jax.random.uniform(offset_key, (3, N_GY, NPS), jnp.float32, -3.0, 3.0)
    placed = jnp.take_along_axis(centers, jnp.broadcast_to(leaf[None], (3, N_GY, NPS)), axis=2)
    return placed + offset


def draw_neighbours(key, part):
    moves = jax.random.randint(jax.random.fold_in(key, 404), (N_GY, K_NB - 1, NLS), -L_DEV, L_DEV + 1)
    leaf = jnp.arange(NLS, dtype=jnp.int32)
    others = jnp.clip(leaf + moves, 0, NLS - 1).astype(jnp.int32)
    return jnp.concatenate([jnp.broadcast_to(leaf, (N_GY, 1, NLS)), others], axis=1)


def draw_inter_leaf(key, part):
    moves = jax.random.randint(jax.random.fold_in(key, 454), (N_GY, K_IL, NLS), -L_DEV, L_DEV + 1)
    leaf = jnp.arange(NLS, dtype=jnp.int32)
    return jnp.clip(leaf + moves, 0, NLS - 1).astype(jnp.int32)


def draw_coarse_op(key, part):
    chosen = jax.random.randint(jax.random.fold_in(key, 505), (N_GY, N_GX, N_GX * N_GY), 0, NOPS)
    boxes = jnp.arange(N_GX * N_GY, dtype=jnp.int32)
    box_owner = boxes // N_GY
    box_slab = boxes % N_GY
    target_slab = jnp.arange(N_GY, dtype=jnp.int32)[:, None, None]
    target_owner = jnp.arange(N_GX, dtype=jnp.int32)[None, :, None]
    close = (box_slab[None, None, :] == target_slab) & (jnp.abs(box_owner[None, None, :] - target_owner) <= 1)
    return jnp.where(close, NOPS, chosen).astype(jnp.int32)


def touch_ends(values, stream_key, least, high):
    longest = values.shape.index(max(values.shape))
    spots = []
    for shift in (0, 1):
        where = [jax.random.randint(jax.random.fold_in(stream_key, axis), (), 0, length) for axis, length in enumerate(values.shape)]
        where[longest] = (where[longest] + shift) % values.shape[longest]
        spots.append(tuple(where))
    return values.at[spots[0]].set(least).at[spots[1]].set(high)


def steps_of(key, dims, cuts, least, top_value):
    def one(axis_at, parts):
        steps = jax.random.uniform(jax.random.fold_in(jax.random.fold_in(key, 6), axis_at), (parts,), jnp.float32, least / len(cuts), top_value / len(cuts))
        return jnp.repeat(jnp.exp(steps), dims[axis_at] // parts).reshape((-1,) + (1,) * (len(dims) - axis_at - 1))

    factor_of = one(*cuts[0])
    for cut in cuts[1:]:
        factor_of = factor_of * one(*cut)
    return factor_of


def noise(own_key, shape, scale, most, cuts=(), kind=jnp.bfloat16):
    factor_of = steps_of(own_key, shape, cuts, -0.22, 0.18) if cuts else 1.0
    values = jax.random.normal(own_key, shape, jnp.float32) * scale * factor_of
    return jnp.minimum(jnp.maximum(values, -most), most).astype(kind)


def setup_inputs(seed: int = 0) -> dict:
    arg_keys = jax.random.split(jax.random.key(seed), 15)
    return {
        "positions": draw_positions(jax.random.fold_in(arg_keys[14], 71), 0),
        "forces": noise(arg_keys[1], (3, N_GY, NPS), 1.0, 6.0, ((1, 2), (2, 16)), jnp.float32),
        "deriv_mat": noise(arg_keys[2], (P_SIZE, P_SIZE), P_SIZE ** -0.5, 0.25, (), jnp.float32),
        "quad_mat": noise(arg_keys[3], (P_SIZE, P_SIZE), P_SIZE ** -0.5, 0.25, (), jnp.float32),
        "point_dest": draw_point_dest(jax.random.fold_in(arg_keys[14], 71), 0),
        "leaf_center": draw_leaf_center(jax.random.fold_in(arg_keys[14], 71), 0),
        "tile_src": draw_tile_src(jax.random.fold_in(arg_keys[14], 71), 0),
        "neighbours": draw_neighbours(jax.random.fold_in(arg_keys[14], 71), 0),
        "inter_leaf": draw_inter_leaf(jax.random.fold_in(arg_keys[14], 71), 0),
        "inter_op": touch_ends(jax.random.randint(arg_keys[9], (N_GY, K_IL, NLS), 0, NOPS), jax.random.fold_in(arg_keys[9], 1), 0, NOPS - 1).astype(jnp.int32),
        "coarse_op": draw_coarse_op(jax.random.fold_in(arg_keys[14], 71), 0),
        "up_pinv": noise(arg_keys[11], (EXP, EXP), EXP ** -0.5, 0.5, (), jnp.float32),
        "trans_ops": noise(arg_keys[12], (NOPS, EXP, EXP), (3 * EXP) ** -0.5, 0.25, (), jnp.float32),
        "child_ops": noise(arg_keys[13], (8, EXP, EXP), (EXP * L_DEV) ** -0.5, 0.03125, (), jnp.float32),
    }


SOFTENING = 0.25
RADIUS = 2.5
HIGHEST = lax.Precision.HIGHEST

def sphere_points(count):
    index = jnp.arange(count).astype(jnp.float32)
    height = 1.0 - (2.0 * index + 1.0) / count
    radial = jnp.sqrt(1.0 - height * height)
    angle = 2.399963 * index
    return jnp.stack([radial * jnp.cos(angle), radial * jnp.sin(angle), height])

def stokes_sum(targets, sources, strengths):
    delta_x = targets[0][:, :, None] - sources[0][:, None, :]
    delta_y = targets[1][:, :, None] - sources[1][:, None, :]
    delta_z = targets[2][:, :, None] - sources[2][:, None, :]
    soft_sq = delta_x * delta_x + delta_y * delta_y + delta_z * delta_z + SOFTENING
    inverse = 1.0 / (soft_sq * jnp.sqrt(soft_sq))
    push_x = strengths[0][:, None, :]
    push_y = strengths[1][:, None, :]
    push_z = strengths[2][:, None, :]
    projected = (push_x * delta_x + push_y * delta_y + push_z * delta_z) * inverse
    direct = (soft_sq + SOFTENING) * inverse
    return jnp.stack([lax.optimization_barrier(jnp.sum(push_x * direct + projected * delta_x, axis=2)), lax.optimization_barrier(jnp.sum(push_y * direct + projected * delta_y, axis=2)), lax.optimization_barrier(jnp.sum(push_z * direct + projected * delta_z, axis=2))])

def by_blocks(func, arrays, total, width):

    def one_block(start):
        return func(*[lax.dynamic_slice_in_dim(item, start, width, 1) for item in arrays])
    starts = (jnp.arange(total // width) * width).astype(jnp.int32)
    result = lax.map(one_block, starts)
    return jnp.transpose(result, (1, 0, 2, 3)).reshape(result.shape[1], total, result.shape[3])

def moments(tiles, centers, sphere, up_pinv, width):
    total = centers.shape[1]
    checks = centers[:, :, None] + RADIUS * sphere[:, None, :]
    values = by_blocks(stokes_sum, [checks, tiles[:3], tiles[3:]], total, width)
    stacked = jnp.transpose(values, (0, 2, 1)).reshape(-1, total)
    return jnp.dot(up_pinv.T, stacked, precision=HIGHEST, preferred_element_type=jnp.float32)

def children(multipole, child_ops):
    expansion = multipole.shape[0]
    grouped = lax.optimization_barrier(jnp.sum(multipole.reshape(expansion, -1, L_DEV // 8, 8), axis=2))
    return jnp.einsum('cef,ebc->bf', child_ops, grouped, precision=HIGHEST)

def coarse_terms(op_rows, coarse):
    onehot = (op_rows[:, :, None] == jnp.arange(NOPS)[None, None, :]).astype(jnp.float32)
    return jnp.einsum('tbk,be->tke', onehot, coarse, precision=HIGHEST)

def translate(trans_ops, grouped):
    return jnp.einsum('kef,tke->tf', trans_ops, grouped, precision=HIGHEST)

def leaf_translate(extended, index, op_rows, trans_ops):
    picked = extended[:, index]
    onehot = (op_rows[:, :, None] == jnp.arange(NOPS)[None, None, :]).astype(jnp.float32)
    grouped = jnp.einsum('ejn,jnk->ken', picked, onehot, precision=HIGHEST)
    return jnp.einsum('kef,ken->fn', trans_ops, grouped, precision=HIGHEST)

def downward(coarse_local, child_ops, leaves):
    pushed = jnp.einsum('cfe,be->fbc', child_ops, coarse_local, precision=HIGHEST)
    expansion = pushed.shape[0]
    boxes = pushed.shape[1]
    spread = jnp.broadcast_to(pushed[:, :, None, :], (expansion, boxes, leaves // 8, 8))
    return spread.reshape(expansion, boxes * leaves)

def evaluate(tiles, centers, sphere, local, width):
    total = centers.shape[1]
    surface = centers[:, :, None] + RADIUS * sphere[:, None, :]
    density = jnp.transpose(local.reshape(3, -1, total), (0, 2, 1))
    return by_blocks(stokes_sum, [tiles[:3], surface, density], total, width)

def route(packed_slab, dest, table):
    source = packed_slab.reshape(6, N_GX, NPD)

    def fill(data, where):
        return jnp.zeros((6, N_GX * CAP), jnp.float32).at[:, where].set(data)
    sent = jax.vmap(fill, in_axes=(1, 0), out_axes=1)(source, dest.reshape(N_GX, NPD))
    sent = sent.reshape(6, N_GX, N_GX, CAP)
    received = jnp.transpose(sent, (0, 2, 1, 3)).reshape(6, N_GX, N_GX * CAP)
    received = jnp.concatenate([received, jnp.zeros((6, N_GX, 1), jnp.float32)], axis=2)
    rows = table.reshape(N_GX, L_DEV * TILE)
    tiles = jnp.take_along_axis(received, jnp.broadcast_to(rows[None], (6,) + rows.shape), axis=2)
    return tiles.reshape(6, NLS, TILE)

def unroute(flow, dest, table):
    rows = table.reshape(N_GX, L_DEV * TILE)
    per_owner = flow.reshape(3, N_GX, L_DEV * TILE)

    def place(values, where):
        return jnp.zeros((3, N_GX * CAP + 1), jnp.float32).at[:, where].set(values)[:, :N_GX * CAP]
    back = jax.vmap(place, in_axes=(1, 0), out_axes=1)(per_owner, rows)
    back = jnp.transpose(back.reshape(3, N_GX, N_GX, CAP), (0, 2, 1, 3)).reshape(3, N_GX, N_GX * CAP)
    where = dest.reshape(N_GX, NPD)
    points = jnp.take_along_axis(back, jnp.broadcast_to(where[None], (3,) + where.shape), axis=2)
    return points.reshape(3, NPS)

def reference(positions, forces, deriv_mat, quad_mat, point_dest, leaf_center, tile_src, neighbours, inter_leaf, inter_op, coarse_op, up_pinv, trans_ops, child_ops):
    tangent = jnp.dot(positions.reshape(-1, P_SIZE), deriv_mat, precision=HIGHEST, preferred_element_type=jnp.float32).reshape(positions.shape)
    jacobian = jnp.sqrt(1.0 + lax.optimization_barrier(jnp.sum(tangent * tangent, axis=0)))
    weighted = jnp.dot(forces.reshape(-1, P_SIZE), quad_mat, precision=HIGHEST, preferred_element_type=jnp.float32).reshape(forces.shape)
    packed = jnp.concatenate([positions, weighted * jacobian[None]], axis=0)
    sphere = sphere_points(SURF)
    width = 64
    tile_sets = []
    multipoles = []
    for slab in range(N_GY):
        tiles = route(packed[:, slab], point_dest[slab], tile_src[slab])
        tile_sets.append(tiles)
        multipoles.append(moments(tiles, leaf_center[:, slab], sphere, up_pinv, width))
    coarse = jnp.stack([children(item, child_ops) for item in multipoles], axis=1).reshape(-1, EXP)
    outputs = []
    for slab in range(N_GY):
        tiles = tile_sets[slab]
        picked = tiles[:, neighbours[slab].T].reshape(6, NLS, -1)
        near = by_blocks(stokes_sum, [tiles[:3], picked[:3], picked[3:]], NLS, width)
        local = leaf_translate(multipoles[slab], inter_leaf[slab], inter_op[slab], trans_ops)
        coarse_local = translate(trans_ops, coarse_terms(coarse_op[slab], coarse))
        local = local + downward(coarse_local, child_ops, L_DEV)
        far = evaluate(tiles, leaf_center[:, slab], sphere, local, width)
        flow = ((near + far) / (8.0 * math.pi)).reshape(3, -1)
        outputs.append(unroute(flow, point_dest[slab], tile_src[slab]))
    return jnp.stack(outputs, axis=1)
```

```python
import functools
import math

import jax
import jax.numpy as jnp
from jax import lax
from jax.experimental import pallas as pl
from jax.experimental.pallas import tpu as pltpu
from jax.sharding import PartitionSpec as P

P_SIZE = 544
NOPS = 16
TILE = 128
L_DEV = 256


SOFTENING = 0.25
RADIUS = 2.5
HIGHEST = lax.Precision.HIGHEST


def extended_2(shard, sides, width):
    for axis, dim in sides:
        devices, length = (lax.axis_size(axis), shard.shape[dim])
        up = [(i, (i + 1) % devices) for i in range(devices - 1)]
        down = [(j, i) for i, j in up]
        last = lax.slice_in_dim(shard, length - width, length, axis=dim)
        first = lax.slice_in_dim(shard, 0, width, axis=dim)
        before = lax.ppermute(last, axis, up)
        after = lax.ppermute(first, axis, down)
        shard = jnp.concatenate([before, shard, after], axis=dim)
    return shard


def sphere_points(count):
    index = jnp.arange(count).astype(jnp.float32)
    height = 1.0 - (2.0 * index + 1.0) / count
    radial = jnp.sqrt(1.0 - height * height)
    angle = 2.399963 * index
    return jnp.stack([radial * jnp.cos(angle), radial * jnp.sin(angle), height])


LANES = 128
ROWS = 8
F32 = jnp.float32
BF16 = jnp.bfloat16
PARAMS = pltpu.CompilerParams(vmem_limit_bytes=48 * 1024 * 1024)


def split_two(value):
    high = value.astype(BF16)
    return high, (value - high.astype(F32)).astype(BF16)


def split_three(value):
    high = value.astype(BF16).astype(F32)
    rest = value - high
    middle = rest.astype(BF16).astype(F32)
    return high, middle, rest - middle


def relative(tile, center):
    row = lax.broadcasted_iota(jnp.int32, tile.shape, 0)
    shift = jnp.where(row == 0, center[0], jnp.where(row == 1, center[1], center[2]))
    return jnp.where(row < 3, tile - shift, 0.0)


def target_rows(pos):
    row = lax.broadcasted_iota(jnp.int32, pos.shape, 0)
    norm = jnp.sum(pos * pos, axis=0, keepdims=True)
    one, two, three = split_three(jnp.where(row == 3, norm, jnp.where(row == 4, 1.0, pos)))
    return jnp.concatenate([one, one, one, two, two, three], axis=0).astype(BF16)


def source_rows(pos):
    row = lax.broadcasted_iota(jnp.int32, pos.shape, 0)
    norm = jnp.sum(pos * pos, axis=0, keepdims=True) + SOFTENING
    one, two, three = split_three(jnp.where(row == 3, 1.0, jnp.where(row == 4, norm, -2.0 * pos)))
    return jnp.concatenate([one, two, three, one, two, one], axis=0).astype(BF16)


def strength_rows(pos, push):
    along = jnp.sum(push * pos[:3], axis=0, keepdims=True)
    first = jnp.concatenate([push, along, along * pos[:3], jnp.zeros_like(along)], axis=0)
    others = [push[k : k + 1] * pos for k in range(3)]
    return jnp.concatenate([first] + others, axis=0)


def pair_sum(target, source, push):
    contract = (((0,), (0,)), ((), ()))
    soft_sq = lax.dot_general(
        source_rows(source), target_rows(target), contract, preferred_element_type=F32
    )
    root = lax.rsqrt(soft_sq)
    inv_high, inv_low = split_two(root * root * root)
    root_high, root_low = split_two(root)
    high, low = split_two(strength_rows(source, push))
    both = jnp.concatenate([high, low], axis=0)
    top = jnp.concatenate([high[:16], low[:16]], axis=0)
    cubed = jnp.dot(both, inv_high, preferred_element_type=F32)
    cubed = cubed[:32] + cubed[32:] + jnp.dot(high, inv_low, preferred_element_type=F32)
    plain = jnp.dot(top, root_high, preferred_element_type=F32)
    plain = plain[:16] + plain[16:] + jnp.dot(high[:16], root_low, preferred_element_type=F32)
    at = target[:3]
    pushed = cubed[:3]
    total = plain[:3] + SOFTENING * pushed + cubed[4:7]
    total = total + at * (jnp.sum(at * pushed, axis=0, keepdims=True) - cubed[3:4])
    for k in range(3):
        total = total - at[k : k + 1] * cubed[8 + 8 * k : 11 + 8 * k]
    return total


def center_of(center_ref, leaf):
    return [center_ref[c, leaf] for c in range(3)]


def near_kernel(center_ref, index_ref, tiles_ref, out_ref):
    lists = index_ref.shape[0]
    for i in range(ROWS):
        leaf = pl.program_id(0) * ROWS + i
        center = center_of(center_ref, leaf)
        own = [tiles_ref[index_ref[n, leaf]] for n in range(lists)]
        points = [relative(tile, center) for tile in own]
        source = jnp.concatenate(points, axis=1)
        push = jnp.concatenate([tile[3:6] for tile in own], axis=1)
        total = pair_sum(points[0], source, push)
        for c in range(3):
            out_ref[c, i : i + 1, :] = total[c : c + 1]


def near_field(center, index, extended):
    leaves = center.shape[1]
    return pl.pallas_call(
        near_kernel,
        grid_spec=pltpu.PrefetchScalarGridSpec(
            num_scalar_prefetch=2,
            grid=(leaves // ROWS,),
            in_specs=[pl.BlockSpec(extended.shape, lambda s, *_: (0, 0, 0))],
            out_specs=pl.BlockSpec((3, ROWS, LANES), lambda s, *_: (0, s, 0)),
        ),
        out_shape=jax.ShapeDtypeStruct((3, leaves, LANES), F32),
        compiler_params=PARAMS,
        name="near_field",
    )(center, index, extended)


def check_kernel(center_ref, tiles_ref, surface_ref, out_ref):
    for i in range(ROWS):
        center = center_of(center_ref, pl.program_id(0) * ROWS + i)
        tile = tiles_ref[i]
        total = pair_sum(surface_ref[...], relative(tile, center), tile[3:6])
        for c in range(3):
            out_ref[c, i : i + 1, :] = total[c : c + 1]


def check_values(center, tiles, surface):
    leaves = center.shape[1]
    return pl.pallas_call(
        check_kernel,
        grid_spec=pltpu.PrefetchScalarGridSpec(
            num_scalar_prefetch=1,
            grid=(leaves // ROWS,),
            in_specs=[
                pl.BlockSpec((ROWS, ROWS, LANES), lambda s, *_: (s, 0, 0)),
                pl.BlockSpec((ROWS, LANES), lambda s, *_: (0, 0)),
            ],
            out_specs=pl.BlockSpec((3, ROWS, LANES), lambda s, *_: (0, s, 0)),
        ),
        out_shape=jax.ShapeDtypeStruct((3, leaves, LANES), F32),
        compiler_params=PARAMS,
        name="check_values",
    )(center, tiles, surface)


def far_kernel(center_ref, tiles_ref, surface_ref, local_ref, near_ref, out_ref):
    for i in range(ROWS):
        center = center_of(center_ref, pl.program_id(0) * ROWS + i)
        push = jnp.concatenate([local_ref[c, i : i + 1, :] for c in range(3)], axis=0)
        total = pair_sum(relative(tiles_ref[i], center), surface_ref[...], push)
        for c in range(3):
            both = near_ref[c, i : i + 1, :] + total[c : c + 1]
            out_ref[c, i : i + 1, :] = both * (1.0 / (8.0 * math.pi))


def far_field(center, tiles, surface, local, near):
    leaves = center.shape[1]
    rows_spec = pl.BlockSpec((3, ROWS, LANES), lambda s, *_: (0, s, 0))
    return pl.pallas_call(
        far_kernel,
        grid_spec=pltpu.PrefetchScalarGridSpec(
            num_scalar_prefetch=1,
            grid=(leaves // ROWS,),
            in_specs=[
                pl.BlockSpec((ROWS, ROWS, LANES), lambda s, *_: (s, 0, 0)),
                pl.BlockSpec((ROWS, LANES), lambda s, *_: (0, 0)),
                rows_spec,
                rows_spec,
            ],
            out_specs=rows_spec,
        ),
        out_shape=jax.ShapeDtypeStruct((3, leaves, LANES), F32),
        compiler_params=PARAMS,
        name="far_field",
    )(center, tiles, surface, local, near)


def scatter_kernel(where_ref, value_ref, out_ref, total_ref):
    parts, kinds, rows, _ = out_ref.shape
    where = where_ref[...]
    high_at, low_at = where >> 7, where & 127
    rows_iota = lax.broadcasted_iota(jnp.int32, (parts * rows, LANES), 0)
    lane_iota = lax.broadcasted_iota(jnp.int32, (LANES, LANES), 0)
    chosen = [rows_iota == high_at[i : i + 1] for i in range(ROWS)]
    onehot = jnp.concatenate([jnp.where(x, 1.0, 0.0).astype(BF16) for x in chosen], axis=1)
    lanes = [lane_iota == low_at[i : i + 1] for i in range(ROWS)]

    @pl.when(pl.program_id(0) == 0)
    def _():
        total_ref[...] = jnp.zeros_like(total_ref)

    for c in range(kinds):
        pieces = split_three(value_ref[c])
        spread = [
            jnp.concatenate(
                [jnp.where(lanes[i], x[i : i + 1], 0.0).astype(BF16) for i in range(ROWS)], axis=1
            )
            for x in pieces
        ]
        for pair in (spread[:2], spread[2:]):
            got = lax.dot_general(
                onehot,
                jnp.concatenate(pair, axis=0) if len(pair) > 1 else pair[0],
                (((1,), (1,)), ((), ())),
                preferred_element_type=F32,
            )
            for k in range(len(pair)):
                total_ref[c] += got[:, k * LANES : (k + 1) * LANES]

    @pl.when(pl.program_id(0) == pl.num_programs(0) - 1)
    def _():
        for part in range(parts):
            for c in range(kinds):
                out_ref[part, c] = total_ref[c, part * rows : (part + 1) * rows]


def scatter_rows(values, where, parts, rows):
    kinds, count = values.shape[:2]
    shape = (parts, kinds, rows, LANES)
    return pl.pallas_call(
        scatter_kernel,
        grid=(count // ROWS,),
        in_specs=[
            pl.BlockSpec((ROWS, LANES), lambda s: (s, 0)),
            pl.BlockSpec((kinds, ROWS, LANES), lambda s: (0, s, 0)),
        ],
        out_specs=pl.BlockSpec(shape, lambda s: (0, 0, 0, 0)),
        out_shape=jax.ShapeDtypeStruct(shape, F32),
        scratch_shapes=[pltpu.VMEM((kinds, parts * rows, LANES), F32)],
        compiler_params=PARAMS,
        name="scatter_rows",
    )(where, values)


def gather_kernel(leaf_major, where_ref, table_ref, out_ref):
    parts, kinds, rows, _ = table_ref.shape
    where = where_ref[...]
    high_at, low_at = where >> 7, where & 127

    def one_part(part, found):
        found = list(found)
        for k in range(rows):
            here = high_at == part * rows + k
            for c in range(kinds):
                line = jnp.broadcast_to(table_ref[part, c, k : k + 1, :], where.shape)
                got = jnp.take_along_axis(line, low_at, axis=1)
                found[c] = jnp.where(here, got, found[c])
        return tuple(found)

    zero = jnp.zeros(where.shape, F32)
    found = lax.fori_loop(0, parts, one_part, (zero,) * kinds)
    if leaf_major:
        for c in range(ROWS):
            out_ref[:, c, :] = found[c] if c < kinds else zero
    else:
        for c in range(kinds):
            out_ref[c] = found[c]


def gather_rows(table, where, leaf_major):
    kinds, count = table.shape[1], where.shape[0]
    if leaf_major:
        shape = (count, ROWS, LANES)
        out_spec = pl.BlockSpec((ROWS, ROWS, LANES), lambda s: (s, 0, 0))
    else:
        shape = (kinds, count, LANES)
        out_spec = pl.BlockSpec((kinds, ROWS, LANES), lambda s: (0, s, 0))
    return pl.pallas_call(
        functools.partial(gather_kernel, leaf_major),
        grid=(count // ROWS,),
        in_specs=[
            pl.BlockSpec((ROWS, LANES), lambda s: (s, 0)),
            pl.BlockSpec(table.shape, lambda s: (0, 0, 0, 0)),
        ],
        out_specs=out_spec,
        out_shape=jax.ShapeDtypeStruct(shape, F32),
        compiler_params=PARAMS,
        name="gather_rows",
    )(where, table)


def gather_boxes(own, axes):
    held = own
    for axis in reversed(axes):
        step = 1
        while step < lax.axis_size(axis):
            pairs = [(i, i ^ step) for i in range(lax.axis_size(axis))]
            other = lax.ppermute(held, axis, pairs)
            upper = (lax.axis_index(axis) // step) % 2 == 1
            held = jnp.where(
                upper,
                jnp.concatenate([other, held], axis=0),
                jnp.concatenate([held, other], axis=0),
            )
            step *= 2
    return held


def pad_rows(array, count, fill):
    wide = ROWS * LANES
    total = -(-count // wide) * wide
    pad = [(0, 0)] * (array.ndim - 1) + [(0, total - count)]
    padded = jnp.pad(array, pad, constant_values=fill)
    return padded.reshape(array.shape[:-1] + (total // LANES, LANES))


def children(multipole, child_ops):
    expansion = multipole.shape[0]
    grouped = jnp.sum(multipole.reshape(expansion, -1, L_DEV // 8, 8), axis=2)
    return jnp.einsum("cef,ebc->bf", child_ops, grouped, precision=HIGHEST)


def coarse_terms(op_rows, coarse):
    onehot = (op_rows[:, :, None] == jnp.arange(NOPS)[None, None, :]).astype(jnp.float32)
    return jnp.einsum("tbk,be->tke", onehot, coarse, precision=HIGHEST)


def translate(trans_ops, grouped):
    return jnp.einsum("kef,tke->tf", trans_ops, grouped, precision=HIGHEST)


def leaf_translate(extended, index, op_rows, trans_ops):
    picked = extended[:, index]
    onehot = (op_rows[:, :, None] == jnp.arange(NOPS)[None, None, :]).astype(jnp.float32)
    grouped = jnp.einsum("ejn,jnk->ken", picked, onehot, precision=HIGHEST)
    return jnp.einsum("kef,ken->fn", trans_ops, grouped, precision=HIGHEST)


def downward(coarse_local, child_ops, leaves):
    pushed = jnp.einsum("cfe,be->fbc", child_ops, coarse_local, precision=HIGHEST)
    expansion = pushed.shape[0]
    boxes = pushed.shape[1]
    spread = jnp.broadcast_to(pushed[:, :, None, :], (expansion, boxes, leaves // 8, 8))
    return spread.reshape(expansion, boxes * leaves)


def body(
    positions,
    forces,
    deriv_mat,
    quad_mat,
    point_dest,
    leaf_center,
    tile_src,
    neighbours,
    inter_leaf,
    inter_op,
    coarse_op,
    up_pinv,
    trans_ops,
    child_ops,
):
    owners = lax.axis_size("gx")
    count = positions.shape[2]
    leaves = leaf_center.shape[2]
    slots = leaves * TILE
    capacity = slots // owners
    tangent = jnp.dot(
        positions.reshape(-1, P_SIZE),
        deriv_mat,
        precision=HIGHEST,
        preferred_element_type=jnp.float32,
    ).reshape(3, count)
    jacobian = jnp.sqrt(1.0 + jnp.sum(tangent * tangent, axis=0))
    weighted = jnp.dot(
        forces.reshape(-1, P_SIZE), quad_mat, precision=HIGHEST, preferred_element_type=jnp.float32
    ).reshape(3, count)
    packed = jnp.concatenate([positions.reshape(3, count), weighted * jacobian[None]], axis=0)
    rows = capacity // LANES
    outgoing = scatter_rows(
        pad_rows(packed, count, 0.0), pad_rows(point_dest[0], count, -1), owners, rows
    )
    first = lax.axis_index("gx") * leaves - leaves
    arrived = lax.all_to_all(outgoing, "gx", split_axis=0, concat_axis=0, tiled=True)
    table = tile_src[0].reshape(leaves, TILE)
    tiles = gather_rows(arrived, table, True)
    extended = extended_2(tiles, (("gx", 0),), leaves)
    points = up_pinv.shape[0] // 3
    surface = jnp.pad(RADIUS * sphere_points(points), ((0, ROWS - 3), (0, LANES - points)))
    centers = leaf_center[:, 0]
    checks = check_values(centers, tiles, surface)[:, :, :points]
    stacked = jnp.transpose(checks, (0, 2, 1)).reshape(3 * points, leaves)
    multipole = jnp.dot(up_pinv.T, stacked, precision=HIGHEST, preferred_element_type=F32)
    multipole_ext = extended_2(multipole, (("gx", 1),), leaves)
    gathered = gather_boxes(children(multipole, child_ops), ("gx", "gy"))
    near = near_field(centers, neighbours[0] - first, extended)
    local = leaf_translate(multipole_ext, inter_leaf[0] - first, inter_op[0], trans_ops)
    grouped = coarse_terms(coarse_op[0], gathered)
    local = local + downward(translate(trans_ops, grouped), child_ops, leaves)
    density = jnp.transpose(local.reshape(3, points, leaves), (0, 2, 1))
    density = jnp.pad(density, ((0, 0), (0, 0), (0, LANES - points)))
    flow = far_field(centers, tiles, surface, density, near)
    returning = scatter_rows(flow, table, owners, rows)
    came_back = lax.all_to_all(returning, "gx", split_axis=0, concat_axis=0, tiled=True)
    found = gather_rows(came_back, pad_rows(point_dest[0], count, 0), False)
    return found.reshape(3, -1)[:, :count].reshape(3, 1, count)


def solution(mesh):
    in_specs = (
        P(None, "gy", "gx"),
        P(None, "gy", "gx"),
        P(),
        P(),
        P("gy", "gx"),
        P(None, "gy", "gx"),
        P("gy", "gx"),
        P("gy", None, "gx"),
        P("gy", None, "gx"),
        P("gy", None, "gx"),
        P("gy", "gx", None),
        P(),
        P(),
        P(),
    )
    out_specs = P(None, "gy", "gx")
    return jax.shard_map(body, mesh=mesh, in_specs=in_specs, out_specs=out_specs, check_vma=False)
```

```python
import functools
import math

import jax
import jax.numpy as jnp
from jax import lax
from jax.experimental import pallas as pl
from jax.experimental.pallas import tpu as pltpu
from jax.sharding import PartitionSpec as P

P_SIZE = 544
NOPS = 16
TILE = 128
L_DEV = 256


SOFTENING = 0.25
RADIUS = 2.5
HIGHEST = lax.Precision.HIGHEST


def extended_2(shard, sides, width):
    for axis, dim in sides:
        devices, length = (lax.axis_size(axis), shard.shape[dim])
        up = [(i, (i + 1) % devices) for i in range(devices - 1)]
        down = [(j, i) for i, j in up]
        last = lax.slice_in_dim(shard, length - width, length, axis=dim)
        first = lax.slice_in_dim(shard, 0, width, axis=dim)
        before = lax.ppermute(last, axis, up)
        after = lax.ppermute(first, axis, down)
        shard = jnp.concatenate([before, shard, after], axis=dim)
    return shard


def sphere_points(count):
    index = jnp.arange(count).astype(jnp.float32)
    height = 1.0 - (2.0 * index + 1.0) / count
    radial = jnp.sqrt(1.0 - height * height)
    angle = 2.399963 * index
    return jnp.stack([radial * jnp.cos(angle), radial * jnp.sin(angle), height])


LANES = 128
ROWS = 8
F32 = jnp.float32
BF16 = jnp.bfloat16
PARAMS = pltpu.CompilerParams(vmem_limit_bytes=48 * 1024 * 1024)


def split_two(value):
    high = value.astype(BF16)
    return high, (value - high.astype(F32)).astype(BF16)


def split_three(value):
    high = value.astype(BF16).astype(F32)
    rest = value - high
    middle = rest.astype(BF16).astype(F32)
    return high, middle, rest - middle


def relative(tile, center):
    row = lax.broadcasted_iota(jnp.int32, tile.shape, 0)
    shift = jnp.where(row == 0, center[0], jnp.where(row == 1, center[1], center[2]))
    return jnp.where(row < 3, tile - shift, 0.0)


def target_rows(pos):
    row = lax.broadcasted_iota(jnp.int32, pos.shape, 0)
    norm = jnp.sum(pos * pos, axis=0, keepdims=True)
    one, two, three = split_three(jnp.where(row == 3, norm, jnp.where(row == 4, 1.0, pos)))
    return jnp.concatenate([one, one, one, two, two, three], axis=0).astype(BF16)


def source_rows(pos):
    row = lax.broadcasted_iota(jnp.int32, pos.shape, 0)
    norm = jnp.sum(pos * pos, axis=0, keepdims=True) + SOFTENING
    one, two, three = split_three(jnp.where(row == 3, 1.0, jnp.where(row == 4, norm, -2.0 * pos)))
    return jnp.concatenate([one, two, three, one, two, one], axis=0).astype(BF16)


def strength_rows(pos, push):
    along = jnp.sum(push * pos[:3], axis=0, keepdims=True)
    first = jnp.concatenate([push, along, along * pos[:3], jnp.zeros_like(along)], axis=0)
    others = [push[k : k + 1] * pos for k in range(3)]
    return jnp.concatenate([first] + others, axis=0)


def pair_sum(target, source, push):
    contract = (((0,), (0,)), ((), ()))
    soft_sq = lax.dot_general(
        source_rows(source), target_rows(target), contract, preferred_element_type=F32
    )
    root = lax.rsqrt(soft_sq)
    inverse = [x.astype(BF16) for x in split_three(root * root * root)]
    root_high, root_low = split_two(root)
    strength = [x.astype(BF16) for x in split_three(strength_rows(source, push))]
    high, low = strength[:2]
    cubed = jnp.zeros((32, target.shape[1]), F32)
    for k in range(3):
        both = jnp.concatenate(strength[: 3 - k], axis=0)
        part = jnp.dot(both, inverse[k], preferred_element_type=F32)
        for j in range(3 - k):
            cubed = cubed + part[32 * j : 32 * j + 32]
    top = jnp.concatenate([high[:16], low[:16]], axis=0)
    plain = jnp.dot(top, root_high, preferred_element_type=F32)
    plain = plain[:16] + plain[16:] + jnp.dot(high[:16], root_low, preferred_element_type=F32)
    at = target[:3]
    pushed = cubed[:3]
    total = plain[:3] + SOFTENING * pushed + cubed[4:7]
    total = total + at * (jnp.sum(at * pushed, axis=0, keepdims=True) - cubed[3:4])
    for k in range(3):
        total = total - at[k : k + 1] * cubed[8 + 8 * k : 11 + 8 * k]
    return total


def center_of(center_ref, leaf):
    return [center_ref[c, leaf] for c in range(3)]


def near_kernel(center_ref, index_ref, tiles_ref, out_ref):
    lists = index_ref.shape[0]
    for i in range(ROWS):
        leaf = pl.program_id(0) * ROWS + i
        center = center_of(center_ref, leaf)
        own = [tiles_ref[index_ref[n, leaf]] for n in range(lists)]
        points = [relative(tile, center) for tile in own]
        source = jnp.concatenate(points, axis=1)
        push = jnp.concatenate([tile[3:6] for tile in own], axis=1)
        total = pair_sum(points[0], source, push)
        for c in range(3):
            out_ref[c, i : i + 1, :] = total[c : c + 1]


def near_field(center, index, extended):
    leaves = center.shape[1]
    return pl.pallas_call(
        near_kernel,
        grid_spec=pltpu.PrefetchScalarGridSpec(
            num_scalar_prefetch=2,
            grid=(leaves // ROWS,),
            in_specs=[pl.BlockSpec(extended.shape, lambda s, *_: (0, 0, 0))],
            out_specs=pl.BlockSpec((3, ROWS, LANES), lambda s, *_: (0, s, 0)),
        ),
        out_shape=jax.ShapeDtypeStruct((3, leaves, LANES), F32),
        compiler_params=PARAMS,
        name="near_field",
    )(center, index, extended)


def check_kernel(center_ref, tiles_ref, surface_ref, out_ref):
    for i in range(ROWS):
        center = center_of(center_ref, pl.program_id(0) * ROWS + i)
        tile = tiles_ref[i]
        total = pair_sum(surface_ref[...], relative(tile, center), tile[3:6])
        for c in range(3):
            out_ref[c, i : i + 1, :] = total[c : c + 1]


def check_values(center, tiles, surface):
    leaves = center.shape[1]
    return pl.pallas_call(
        check_kernel,
        grid_spec=pltpu.PrefetchScalarGridSpec(
            num_scalar_prefetch=1,
            grid=(leaves // ROWS,),
            in_specs=[
                pl.BlockSpec((ROWS, ROWS, LANES), lambda s, *_: (s, 0, 0)),
                pl.BlockSpec((ROWS, LANES), lambda s, *_: (0, 0)),
            ],
            out_specs=pl.BlockSpec((3, ROWS, LANES), lambda s, *_: (0, s, 0)),
        ),
        out_shape=jax.ShapeDtypeStruct((3, leaves, LANES), F32),
        compiler_params=PARAMS,
        name="check_values",
    )(center, tiles, surface)


def far_kernel(center_ref, tiles_ref, surface_ref, local_ref, near_ref, out_ref):
    for i in range(ROWS):
        center = center_of(center_ref, pl.program_id(0) * ROWS + i)
        push = jnp.concatenate([local_ref[c, i : i + 1, :] for c in range(3)], axis=0)
        total = pair_sum(relative(tiles_ref[i], center), surface_ref[...], push)
        for c in range(3):
            both = near_ref[c, i : i + 1, :] + total[c : c + 1]
            out_ref[c, i : i + 1, :] = both * (1.0 / (8.0 * math.pi))


def far_field(center, tiles, surface, local, near):
    leaves = center.shape[1]
    rows_spec = pl.BlockSpec((3, ROWS, LANES), lambda s, *_: (0, s, 0))
    return pl.pallas_call(
        far_kernel,
        grid_spec=pltpu.PrefetchScalarGridSpec(
            num_scalar_prefetch=1,
            grid=(leaves // ROWS,),
            in_specs=[
                pl.BlockSpec((ROWS, ROWS, LANES), lambda s, *_: (s, 0, 0)),
                pl.BlockSpec((ROWS, LANES), lambda s, *_: (0, 0)),
                rows_spec,
                rows_spec,
            ],
            out_specs=rows_spec,
        ),
        out_shape=jax.ShapeDtypeStruct((3, leaves, LANES), F32),
        compiler_params=PARAMS,
        name="far_field",
    )(center, tiles, surface, local, near)


def scatter_kernel(where_ref, value_ref, out_ref, total_ref):
    parts, kinds, rows, _ = out_ref.shape
    where = where_ref[...]
    high_at, low_at = where >> 7, where & 127
    rows_iota = lax.broadcasted_iota(jnp.int32, (parts * rows, LANES), 0)
    lane_iota = lax.broadcasted_iota(jnp.int32, (LANES, LANES), 0)
    chosen = [rows_iota == high_at[i : i + 1] for i in range(ROWS)]
    onehot = jnp.concatenate([jnp.where(x, 1.0, 0.0).astype(BF16) for x in chosen], axis=1)
    lanes = [lane_iota == low_at[i : i + 1] for i in range(ROWS)]

    @pl.when(pl.program_id(0) == 0)
    def _():
        total_ref[...] = jnp.zeros_like(total_ref)

    for c in range(kinds):
        pieces = split_three(value_ref[c])
        spread = [
            jnp.concatenate(
                [jnp.where(lanes[i], x[i : i + 1], 0.0).astype(BF16) for i in range(ROWS)], axis=1
            )
            for x in pieces
        ]
        for pair in (spread[:2], spread[2:]):
            got = lax.dot_general(
                onehot,
                jnp.concatenate(pair, axis=0) if len(pair) > 1 else pair[0],
                (((1,), (1,)), ((), ())),
                preferred_element_type=F32,
            )
            for k in range(len(pair)):
                total_ref[c] += got[:, k * LANES : (k + 1) * LANES]

    @pl.when(pl.program_id(0) == pl.num_programs(0) - 1)
    def _():
        for part in range(parts):
            for c in range(kinds):
                out_ref[part, c] = total_ref[c, part * rows : (part + 1) * rows]


def scatter_rows(values, where, parts, rows):
    kinds, count = values.shape[:2]
    shape = (parts, kinds, rows, LANES)
    return pl.pallas_call(
        scatter_kernel,
        grid=(count // ROWS,),
        in_specs=[
            pl.BlockSpec((ROWS, LANES), lambda s: (s, 0)),
            pl.BlockSpec((kinds, ROWS, LANES), lambda s: (0, s, 0)),
        ],
        out_specs=pl.BlockSpec(shape, lambda s: (0, 0, 0, 0)),
        out_shape=jax.ShapeDtypeStruct(shape, F32),
        scratch_shapes=[pltpu.VMEM((kinds, parts * rows, LANES), F32)],
        compiler_params=PARAMS,
        name="scatter_rows",
    )(where, values)


def gather_kernel(leaf_major, where_ref, table_ref, out_ref):
    parts, kinds, rows, _ = table_ref.shape
    where = where_ref[...]
    high_at, low_at = where >> 7, where & 127

    def one_part(part, found):
        found = list(found)
        for k in range(rows):
            here = high_at == part * rows + k
            for c in range(kinds):
                line = jnp.broadcast_to(table_ref[part, c, k : k + 1, :], where.shape)
                got = jnp.take_along_axis(line, low_at, axis=1)
                found[c] = jnp.where(here, got, found[c])
        return tuple(found)

    zero = jnp.zeros(where.shape, F32)
    found = lax.fori_loop(0, parts, one_part, (zero,) * kinds)
    if leaf_major:
        for c in range(ROWS):
            out_ref[:, c, :] = found[c] if c < kinds else zero
    else:
        for c in range(kinds):
            out_ref[c] = found[c]


def gather_rows(table, where, leaf_major):
    kinds, count = table.shape[1], where.shape[0]
    if leaf_major:
        shape = (count, ROWS, LANES)
        out_spec = pl.BlockSpec((ROWS, ROWS, LANES), lambda s: (s, 0, 0))
    else:
        shape = (kinds, count, LANES)
        out_spec = pl.BlockSpec((kinds, ROWS, LANES), lambda s: (0, s, 0))
    return pl.pallas_call(
        functools.partial(gather_kernel, leaf_major),
        grid=(count // ROWS,),
        in_specs=[
            pl.BlockSpec((ROWS, LANES), lambda s: (s, 0)),
            pl.BlockSpec(table.shape, lambda s: (0, 0, 0, 0)),
        ],
        out_specs=out_spec,
        out_shape=jax.ShapeDtypeStruct(shape, F32),
        compiler_params=PARAMS,
        name="gather_rows",
    )(where, table)


def gather_boxes(own, axes):
    held = own
    for axis in reversed(axes):
        step = 1
        while step < lax.axis_size(axis):
            pairs = [(i, i ^ step) for i in range(lax.axis_size(axis))]
            other = lax.ppermute(held, axis, pairs)
            upper = (lax.axis_index(axis) // step) % 2 == 1
            held = jnp.where(
                upper,
                jnp.concatenate([other, held], axis=0),
                jnp.concatenate([held, other], axis=0),
            )
            step *= 2
    return held


def pad_rows(array, count, fill):
    wide = ROWS * LANES
    total = -(-count // wide) * wide
    pad = [(0, 0)] * (array.ndim - 1) + [(0, total - count)]
    padded = jnp.pad(array, pad, constant_values=fill)
    return padded.reshape(array.shape[:-1] + (total // LANES, LANES))


def children(multipole, child_ops):
    expansion = multipole.shape[0]
    grouped = jnp.sum(multipole.reshape(expansion, -1, L_DEV // 8, 8), axis=2)
    return jnp.einsum("cef,ebc->bf", child_ops, grouped, precision=HIGHEST)


def coarse_terms(op_rows, coarse):
    onehot = (op_rows[:, :, None] == jnp.arange(NOPS)[None, None, :]).astype(jnp.float32)
    return jnp.einsum("tbk,be->tke", onehot, coarse, precision=HIGHEST)


def translate(trans_ops, grouped):
    return jnp.einsum("kef,tke->tf", trans_ops, grouped, precision=HIGHEST)


def leaf_translate(extended, index, op_rows, trans_ops):
    picked = extended[:, index]
    onehot = (op_rows[:, :, None] == jnp.arange(NOPS)[None, None, :]).astype(jnp.float32)
    grouped = jnp.einsum("ejn,jnk->ken", picked, onehot, precision=HIGHEST)
    return jnp.einsum("kef,ken->fn", trans_ops, grouped, precision=HIGHEST)


def downward(coarse_local, child_ops, leaves):
    pushed = jnp.einsum("cfe,be->fbc", child_ops, coarse_local, precision=HIGHEST)
    expansion = pushed.shape[0]
    boxes = pushed.shape[1]
    spread = jnp.broadcast_to(pushed[:, :, None, :], (expansion, boxes, leaves // 8, 8))
    return spread.reshape(expansion, boxes * leaves)


def body(
    positions,
    forces,
    deriv_mat,
    quad_mat,
    point_dest,
    leaf_center,
    tile_src,
    neighbours,
    inter_leaf,
    inter_op,
    coarse_op,
    up_pinv,
    trans_ops,
    child_ops,
):
    owners = lax.axis_size("gx")
    count = positions.shape[2]
    leaves = leaf_center.shape[2]
    slots = leaves * TILE
    capacity = slots // owners
    tangent = jnp.dot(
        positions.reshape(-1, P_SIZE),
        deriv_mat,
        precision=HIGHEST,
        preferred_element_type=jnp.float32,
    ).reshape(3, count)
    jacobian = jnp.sqrt(1.0 + jnp.sum(tangent * tangent, axis=0))
    weighted = jnp.dot(
        forces.reshape(-1, P_SIZE), quad_mat, precision=HIGHEST, preferred_element_type=jnp.float32
    ).reshape(3, count)
    packed = jnp.concatenate([positions.reshape(3, count), weighted * jacobian[None]], axis=0)
    rows = capacity // LANES
    outgoing = scatter_rows(
        pad_rows(packed, count, 0.0), pad_rows(point_dest[0], count, -1), owners, rows
    )
    first = lax.axis_index("gx") * leaves - leaves
    arrived = lax.all_to_all(outgoing, "gx", split_axis=0, concat_axis=0, tiled=True)
    table = tile_src[0].reshape(leaves, TILE)
    tiles = gather_rows(arrived, table, True)
    extended = extended_2(tiles, (("gx", 0),), leaves)
    points = up_pinv.shape[0] // 3
    surface = jnp.pad(RADIUS * sphere_points(points), ((0, ROWS - 3), (0, LANES - points)))
    centers = leaf_center[:, 0]
    checks = check_values(centers, tiles, surface)[:, :, :points]
    stacked = jnp.transpose(checks, (0, 2, 1)).reshape(3 * points, leaves)
    multipole = jnp.dot(up_pinv.T, stacked, precision=HIGHEST, preferred_element_type=F32)
    multipole_ext = extended_2(multipole, (("gx", 1),), leaves)
    gathered = gather_boxes(children(multipole, child_ops), ("gx", "gy"))
    near = near_field(centers, neighbours[0] - first, extended)
    local = leaf_translate(multipole_ext, inter_leaf[0] - first, inter_op[0], trans_ops)
    grouped = coarse_terms(coarse_op[0], gathered)
    local = local + downward(translate(trans_ops, grouped), child_ops, leaves)
    density = jnp.transpose(local.reshape(3, points, leaves), (0, 2, 1))
    density = jnp.pad(density, ((0, 0), (0, 0), (0, LANES - points)))
    flow = far_field(centers, tiles, surface, density, near)
    returning = scatter_rows(flow, table, owners, rows)
    came_back = lax.all_to_all(returning, "gx", split_axis=0, concat_axis=0, tiled=True)
    found = gather_rows(came_back, pad_rows(point_dest[0], count, 0), False)
    return found.reshape(3, -1)[:, :count].reshape(3, 1, count)


def solution(mesh):
    in_specs = (
        P(None, "gy", "gx"),
        P(None, "gy", "gx"),
        P(),
        P(),
        P("gy", "gx"),
        P(None, "gy", "gx"),
        P("gy", "gx"),
        P("gy", None, "gx"),
        P("gy", None, "gx"),
        P("gy", None, "gx"),
        P("gy", "gx", None),
        P(),
        P(),
        P(),
    )
    out_specs = P(None, "gy", "gx")
    return jax.shard_map(body, mesh=mesh, in_specs=in_specs, out_specs=out_specs, check_vma=False)
```
